32 devices in a mesh: parts: 2 (over y), rep: 4 (over x, core), tp: 4 (over z).
Axes of the slice: x: 2, y: 2, z: 4, core: 2. Of those that a mesh axis runs over, the one named last changes fastest.
Arguments:
- tokens: bfloat16 [2048, 8192], P(('parts', 'rep'), 'tp'), parts along dimension 0, may hold values from -6 to 6
- base_output_weight: bfloat16 [8192, 8192], P('tp', 'rep'), may hold values from -0.0625 to 0.0625
- token_adapter_index: int32 [2048], P('parts'), parts along dimension 0, may hold values from 0 to 7
- adapter_rank_block_count: int32 [8], replicated, may hold values from 1 to 8
- adapter_input_factors: bfloat16 [8, 8192, 128], P('rep', 'tp'), may hold values from -0.0625 to 0.0625
- adapter_output_factors: bfloat16 [8, 128, 8192], P('tp', None, 'rep'), may hold values from -0.5 to 0.5
Outputs:
- mixed: bfloat16 [2048, 8192], P(('parts', 'tp'), 'rep'), parts along dimension 0
The draws below stay inside these ranges and needn't reach their ends.
There are 2 independent parts, one for each index of `parts`. The reference program is written for one: setup_inputs(seed, part) draws one part's arguments, and reference() takes and returns one part's arrays. A program takes and returns all parts, laid end to end along the dimension named above; an argument that names none is the same for every part. Nothing has to cross between parts.
All inputs are finite; a program needn't handle non-finite values.
Results may differ from the reference program's by a relative error of at most 0.009.
Values may be sent and summed in bfloat16 or wider, within the bound.
A program may use at most 64 MiB of HBM per device.

```python
import math
import jax
import jax.numpy as jnp
import numpy as np
from jax import lax

MODEL_WIDTH = 8192
PADDED_RANK = 128
RBLK = 16
TOKENS = 1024
ADAPTER_TOTAL = 8
ADP_TP = 2
N_TP = 4


def touch_ends(result, own_key, least, high):
    longest = result.shape.index(max(result.shape))
    spots = []
    for shift in (0, 1):
        where = [jax.random.randint(jax.random.fold_in(own_key, axis), (), 0, length) for axis, length in enumerate(result.shape)]
        where[longest] = (where[longest] + shift) % result.shape[longest]
        spots.append(tuple(where))
    return result.at[spots[0]].set(least).at[spots[1]].set(high)


def level_of(own_key, shape, shards, least, largest):
    def one(dim, blocks):
        heights = jax.random.uniform(jax.random.fold_in(jax.random.fold_in(own_key, 6), dim), (blocks,), jnp.float32, least / len(shards), largest / len(shards))
        return jnp.repeat(jnp.exp(heights), shape[dim] // blocks).reshape((-1,) + (1,) * (len(shape) - dim - 1))

    level = one(*shards[0])
    for cut in shards[1:]:
        level = level * one(*cut)
    return level


def rank_table(amount, slope):
    loads = [(1 << 20) // math.isqrt(grade ** slope) + 1 for grade in range(1, amount + 1)]
    deviation = 1 + sum(loads) // (1 << 30)
    return np.cumsum(np.array([max(1, weight // deviation) for weight in loads]))


def ranked_ids(own_key, dims, number_of, lean):
    listing = rank_table(number_of, lean)
    lot = jax.random.randint(jax.random.fold_in(own_key, 1), dims, 0, int(listing[number_of - 1]))
    standing = jnp.searchsorted(jnp.asarray(listing, jnp.int32), lot, side="right")
    return jax.random.permutation(jax.random.fold_in(own_key, 2), number_of)[standing].astype(jnp.int32)


def normal_values(key, dims, spread, limit, shards=(), dtype=jnp.bfloat16):
    entries = jax.random.normal(key, dims, jnp.float32) * spread
    if len(shards) > 0:
        entries = level_of(key, dims, shards, -0.22, 0.18) * entries
    return jnp.clip(entries, min=-limit, max=limit).astype(dtype)


def setup_inputs(seed: int = 0, part: int = 0) -> dict:
    key_list = jax.random.split(jax.random.key(seed), 7)
    own_keys = jax.random.split(jax.random.fold_in(key_list[6], part), 7)
    tokens = normal_values(own_keys[0], (TOKENS, MODEL_WIDTH), 1.0, 6.0, ((0, 4), (1, 4)))
    base_output_weight = normal_values(key_list[1], (MODEL_WIDTH, MODEL_WIDTH), MODEL_WIDTH ** -0.5, 0.0625, ((0, 4), (1, 4)))
    token_adapter_index = touch_ends(ranked_ids(own_keys[2], (TOKENS,), ADAPTER_TOTAL, 2), jax.random.fold_in(own_keys[2], 3), 0, ADAPTER_TOTAL - 1).astype(jnp.int32)
    adapter_rank_block_count = touch_ends(jax.random.randint(key_list[3], (ADAPTER_TOTAL,), 1, 9), jax.random.fold_in(key_list[3], 1), 1, 8).astype(jnp.int32)
    adapter_input_factors = normal_values(key_list[4], (ADAPTER_TOTAL, MODEL_WIDTH, PADDED_RANK), MODEL_WIDTH ** -0.5, 0.0625, ((0, 4), (1, 4)))
    adapter_output_factors = normal_values(key_list[5], (ADAPTER_TOTAL, PADDED_RANK, MODEL_WIDTH), PADDED_RANK ** -0.5, 0.5, ((0, 4), (2, 4)))
    return dict(tokens=tokens, base_output_weight=base_output_weight, token_adapter_index=token_adapter_index, adapter_rank_block_count=adapter_rank_block_count, adapter_input_factors=adapter_input_factors, adapter_output_factors=adapter_output_factors)


def reference(tokens, base_output_weight, token_adapter_index, adapter_rank_block_count, adapter_input_factors, adapter_output_factors):
    rank = RBLK * adapter_rank_block_count[token_adapter_index]
    keep = jnp.arange(PADDED_RANK)[None, :] < rank[:, None]
    scale = 8.0 / jnp.sqrt(rank.astype(jnp.float32))
    token_blocks = tokens.reshape(TOKENS // 16, 16, MODEL_WIDTH)
    id_blocks = token_adapter_index.reshape(TOKENS // 16, 16)

    def block_lowrank(args):
        rows, adapter_identifiers = args
        adapter_factors = adapter_input_factors[adapter_identifiers].astype(jnp.float32)
        return jnp.einsum('rd,rdk->rk', rows.astype(jnp.float32), adapter_factors)
    lowrank_raw = lax.map(block_lowrank, (token_blocks, id_blocks)).reshape(TOKENS, PADDED_RANK)
    lowrank = jnp.where(keep, lowrank_raw * scale[:, None], 0.0).astype(jnp.bfloat16)

    def block_delta(args):
        rows, adapter_identifiers = args
        adapter_factors = adapter_output_factors[adapter_identifiers].astype(jnp.float32)
        return jnp.einsum('rk,rkc->rc', rows.astype(jnp.float32), adapter_factors)
    delta = lax.map(block_delta, (lowrank.reshape(TOKENS // 16, 16, PADDED_RANK), id_blocks)).reshape(TOKENS, MODEL_WIDTH)
    width = MODEL_WIDTH // N_TP
    total = jnp.zeros((TOKENS, MODEL_WIDTH), jnp.float32)
    for index in range(N_TP):
        part = jnp.dot(tokens[:, index * width:(index + 1) * width], base_output_weight[index * width:(index + 1) * width], preferred_element_type=jnp.float32)
        owned = token_adapter_index // ADP_TP == index
        part = part + jnp.where(owned[:, None], delta, 0.0)
        rounded = lax.optimization_barrier(part.astype(jnp.bfloat16))
        total = total + rounded.astype(jnp.float32)
    return total.astype(jnp.bfloat16)
```

```python
import functools

import jax
import jax.numpy as jnp
from jax import lax
from jax.experimental import pallas as pl
from jax.experimental.pallas import tpu as pltpu
from jax.sharding import PartitionSpec as P

RBLK = 16
STEPS = 4
MESH = pl.DeviceIdType.MESH


def kernel(
    reps,
    tps,
    steps,
    tokens,
    weight,
    factors_in,
    factors_out,
    adapter,
    scale,
    out,
    tok,
    w,
    fin,
    fout,
    base,
    acc,
    up,
    down,
    done,
    ask,
    asked,
    low,
    lows,
    spread,
    load_sem,
    own_sem,
    out_sem,
    tok_send,
    tok_fwd,
    tok_recv,
    a_send,
    a_recv,
    b_send,
    b_recv,
    c_send,
    c_recv,
    up_send,
    up_recv,
    down_send,
    down_recv,
):
    r = lax.axis_index("rep")
    t = lax.axis_index("tp")
    rows = tokens.shape[0]
    q = rows // steps
    width = weight.shape[1]
    tile = min(width, 512)
    in_share, out_share = fin.shape[0], fout.shape[0]
    rank = fin.shape[2]
    f32, bf16 = jnp.float32, jnp.bfloat16
    sibling = r + 1 - 2 * (r % 2)
    peers = [(r + 2 * j) % reps for j in range(1, reps // 2)]

    def remote(src, dst, send, recv, **where):
        return pltpu.make_async_remote_copy(
            src_ref=src, dst_ref=dst, send_sem=send, recv_sem=recv, device_id=where, device_id_type=MESH
        )

    loads = [
        pltpu.make_async_copy(src, dst, load_sem.at[i])
        for i, (src, dst) in enumerate(((factors_in, fin), (weight, w), (factors_out, fout)))
    ]
    for copy in loads:
        copy.start()

    def own(s):
        return pltpu.make_async_copy(tokens.at[pl.ds(s * q, q)], tok.at[s, r], own_sem.at[s])

    for s in range(steps):
        own(s).start()

    barrier = pltpu.get_barrier_semaphore()
    for j in range(1, reps):
        pl.semaphore_signal(barrier, inc=1, device_id={"rep": (r + j) % reps}, device_id_type=MESH)
    for j in range(1, tps):
        pl.semaphore_signal(barrier, inc=1, device_id={"tp": (t + j) % tps}, device_id_type=MESH)
    pl.semaphore_wait(barrier, reps + tps - 2)

    def token_copy(s, block, to, send, from_tokens):
        src = tokens.at[pl.ds(s * q, q)] if from_tokens else tok.at[s, block]
        return remote(src, tok.at[s, block], send, tok_recv.at[s, block], rep=to)

    def gather_start(s):
        for j, peer in enumerate(peers):
            token_copy(s, r, peer, tok_send.at[s, j], True).start()
        token_copy(s, r, sibling, tok_send.at[s, len(peers)], True).start()

    def gather_finish(s):
        own(s).wait()
        for j, peer in enumerate(peers):
            token_copy(s, peer, peer, tok_send.at[s, j], False).wait_recv()
            token_copy(s, peer, sibling, tok_fwd.at[s, j], False).start()
        token_copy(s, sibling, sibling, tok_send.at[s, len(peers)], False).wait_recv()
        for peer in peers:
            other = peer + 1 - 2 * (peer % 2)
            token_copy(s, other, sibling, tok_send.at[s, 0], False).wait_recv()

    def lowrank_ask(s):
        rowsall = tok[s].reshape(reps * q, tok.shape[3])
        chosen = jnp.zeros((reps * q, rank), f32)
        wanted = adapter[s].reshape(reps * q, rank) - r * in_share
        for n in range(in_share):
            product = jnp.dot(rowsall, fin[n], preferred_element_type=f32)
            chosen = jnp.where(wanted == n, product, chosen)
        ask[s] = chosen.astype(bf16).reshape(reps, q, rank)
        for j in range(1, reps):
            a_copy(s, (r + j) % reps, r, j).start()

    def a_copy(s, to, slot, j):
        return remote(ask.at[s, to], asked.at[s, slot], a_send.at[s, j], a_recv.at[s, slot], rep=to)

    def lowrank_sum(s):
        total = ask[s, r].astype(f32)
        for j in range(1, reps):
            peer = (r + j) % reps
            a_copy(s, peer, peer, j).wait_recv()
            total += asked[s, peer].astype(f32)
        lows[s, t] = total.astype(bf16)
        for j in range(1, tps):
            b_copy(s, (t + j) % tps, t, j).start()

    def b_copy(s, to, slot, j):
        return remote(lows.at[s, slot], lows.at[s, slot], b_send.at[s, j], b_recv.at[s, slot], tp=to)

    def lowrank_scale(s):
        for j in range(1, tps):
            peer = (t + j) % tps
            b_copy(s, peer, peer, j).wait_recv()
        total = lows[s, 0].astype(f32)
        for k in range(1, tps):
            total += lows[s, k].astype(f32)
        low[s, r] = (total * scale[s, r]).astype(bf16)
        for j in range(1, reps):
            c_copy(s, (r + j) % reps, r, j).start()

    def c_copy(s, to, slot, j):
        return remote(low.at[s, slot], low.at[s, slot], c_send.at[s, j], c_recv.at[s, slot], rep=to)

    def lowrank_wait(s):
        for j in range(1, reps):
            peer = (r + j) % reps
            c_copy(s, peer, peer, j).wait_recv()

    def project(s):
        @pl.loop(0, width // tile)
        def _(i):
            columns = pl.ds(pl.multiple_of(i * tile, tile), tile)
            base[:, columns] = jnp.dot(
                tok[s].reshape(reps * q, tok.shape[3]), w[:, columns], preferred_element_type=f32
            )

    def adapt(s):
        mine = adapter[s].reshape(reps * q, rank) - t * out_share
        value = low[s].reshape(reps * q, rank)
        for n in range(out_share):
            spread[:, n * rank : (n + 1) * rank] = jnp.where(
                mine == n, value.astype(f32), 0.0
            ).astype(bf16)

        @pl.loop(0, width // tile)
        def _(i):
            columns = pl.ds(pl.multiple_of(i * tile, tile), tile)
            block = fout[:, :, columns].reshape(out_share * rank, tile)
            delta = jnp.dot(spread[...], block, preferred_element_type=f32)
            acc[s, :, :, columns] = (base[:, columns] + delta).astype(bf16).reshape(tps, q, tile)

    def up_copy(s, src, b, to):
        return remote(src.at[s, b], up.at[s, b], up_send.at[s, b], up_recv.at[s, b], tp=to)

    def down_copy(s, src, b, to):
        return remote(src.at[s, b], down.at[s, b], down_send.at[s, b], down_recv.at[s, b], tp=to)

    above = jnp.minimum(t + 1, tps - 1)
    below = jnp.maximum(t - 1, 0)

    def ends_send(s):
        @pl.when(t == 0)
        def _():
            for b in range(tps - 1, 0, -1):
                up_copy(s, acc, b, 1).start()

        @pl.when(t == tps - 1)
        def _():
            for b in range(tps - 1):
                down_copy(s, acc, b, tps - 2).start()

    def write(s):
        return pltpu.make_async_copy(done.at[s], out.at[pl.ds(s * q, q)], out_sem.at[s])

    def pass_on(s):
        for j in range(tps):
            b = tps - 1 - j

            @pl.when((t > 0) & (b > t))
            def _():
                up_copy(s, up, b, t - 1).wait_recv()
                up[s, b] = (up[s, b].astype(f32) + acc[s, b].astype(f32)).astype(bf16)
                up_copy(s, up, b, t + 1).start()

            @pl.when((t < tps - 1) & (j < t))
            def _():
                down_copy(s, down, j, t + 1).wait_recv()
                down[s, j] = (down[s, j].astype(f32) + acc[s, j].astype(f32)).astype(bf16)
                down_copy(s, down, j, t - 1).start()

        @pl.when(t == 0)
        def _():
            down_copy(s, down, 0, 1).wait_recv()
            done[s] = (acc[s, 0].astype(f32) + down[s, 0].astype(f32)).astype(bf16)

        @pl.when(t == tps - 1)
        def _():
            up_copy(s, up, tps - 1, tps - 2).wait_recv()
            done[s] = (acc[s, tps - 1].astype(f32) + up[s, tps - 1].astype(f32)).astype(bf16)

        @pl.when((t > 0) & (t < tps - 1))
        def _():
            up_copy(s, up, t, t - 1).wait_recv()
            down_copy(s, down, t, t + 1).wait_recv()
            done[s] = (
                acc[s, t].astype(f32) + up[s, t].astype(f32) + down[s, t].astype(f32)
            ).astype(bf16)

        write(s).start()

    gather_start(0)
    loads[0].wait()
    gather_finish(0)
    if steps > 1:
        gather_start(1)
    lowrank_ask(0)
    loads[1].wait()
    project(0)
    lowrank_sum(0)
    lowrank_scale(0)
    loads[2].wait()
    for s in range(steps):
        more = s + 1 < steps
        if more:
            gather_finish(s + 1)
            if s + 2 < steps:
                gather_start(s + 2)
            lowrank_ask(s + 1)
        lowrank_wait(s)
        adapt(s)
        if more:
            lowrank_sum(s + 1)
        ends_send(s)
        if more:
            project(s + 1)
            lowrank_scale(s + 1)
        if s > 0:
            pass_on(s - 1)
    pass_on(steps - 1)

    for s in range(steps):
        for j, peer in enumerate(peers):
            token_copy(s, r, peer, tok_send.at[s, j], True).wait_send()
            token_copy(s, peer, sibling, tok_fwd.at[s, j], False).wait_send()
        token_copy(s, r, sibling, tok_send.at[s, len(peers)], True).wait_send()
        for j in range(1, reps):
            a_copy(s, (r + j) % reps, r, j).wait_send()
            c_copy(s, (r + j) % reps, r, j).wait_send()
        for j in range(1, tps):
            b_copy(s, (t + j) % tps, t, j).wait_send()
        for b in range(tps):

            @pl.when(b > t)
            def _():
                up_copy(s, up, b, t + 1).wait_send()

            @pl.when(b < t)
            def _():
                down_copy(s, down, b, t - 1).wait_send()

        write(s).wait()


def body(reps, tps, tokens, weight, token_adapter_index, block_count, factors_in, factors_out):
    rows, depth = tokens.shape
    width = weight.shape[1]
    in_share, _, rank = factors_in.shape
    out_share = factors_out.shape[0]
    steps = STEPS
    q = rows // steps
    table = token_adapter_index[:, None] == jnp.arange(block_count.shape[0])[None, :]
    ranks = RBLK * jnp.sum(jnp.where(table, block_count[None, :], 0), axis=1)
    keep = jnp.arange(rank)[None, :] < ranks[:, None]
    scale = jnp.where(keep, (8.0 / jnp.sqrt(ranks.astype(jnp.float32)))[:, None], 0.0)
    adapter = jnp.broadcast_to(token_adapter_index[:, None], scale.shape)

    def by_step(x):
        return x.reshape(reps, steps, q, rank).transpose(1, 0, 2, 3)

    vmem = pl.BlockSpec(memory_space=pltpu.VMEM)
    hbm = pl.BlockSpec(memory_space=pl.ANY)
    f32, bf16 = jnp.float32, jnp.bfloat16
    dma = pltpu.SemaphoreType.DMA
    return pl.pallas_call(
        functools.partial(kernel, reps, tps, steps),
        out_shape=jax.ShapeDtypeStruct((rows, width), bf16),
        in_specs=[hbm, hbm, hbm, hbm, vmem, vmem],
        out_specs=hbm,
        scratch_shapes=[
            pltpu.VMEM((steps, reps, q, depth), bf16),
            pltpu.VMEM(weight.shape, bf16),
            pltpu.VMEM(factors_in.shape, bf16),
            pltpu.VMEM(factors_out.shape, bf16),
            pltpu.VMEM((reps * q, width), f32),
            pltpu.VMEM((steps, tps, q, width), bf16),
            pltpu.VMEM((steps, tps, q, width), bf16),
            pltpu.VMEM((steps, tps, q, width), bf16),
            pltpu.VMEM((steps, q, width), bf16),
            pltpu.VMEM((steps, reps, q, rank), bf16),
            pltpu.VMEM((steps, reps, q, rank), bf16),
            pltpu.VMEM((steps, reps, q, rank), bf16),
            pltpu.VMEM((steps, tps, q, rank), bf16),
            pltpu.VMEM((reps * q, out_share * rank), bf16),
            dma((3,)),
            dma((steps,)),
            dma((steps,)),
            dma((steps, reps)),
            dma((steps, reps)),
            dma((steps, reps)),
            dma((steps, reps)),
            dma((steps, reps)),
            dma((steps, tps)),
            dma((steps, tps)),
            dma((steps, reps)),
            dma((steps, reps)),
            dma((steps, tps)),
            dma((steps, tps)),
            dma((steps, tps)),
            dma((steps, tps)),
        ],
        compiler_params=pltpu.CompilerParams(
            collective_id=0, has_side_effects=True, vmem_limit_bytes=48 << 20
        ),
    )(tokens, weight, factors_in, factors_out, by_step(adapter), by_step(scale))


def solution(mesh):
    placed = (
        P(("parts", "rep"), "tp"),
        P("tp", "rep"),
        P("parts"),
        P(),
        P("rep", "tp", None),
        P("tp", None, "rep"),
    )
    return jax.shard_map(
        functools.partial(body, mesh.shape["rep"], mesh.shape["tp"]),
        mesh=mesh,
        in_specs=placed,
        out_specs=P(("parts", "tp"), "rep"),
        check_vma=False,
    )
```

```python
import functools

import jax
import jax.numpy as jnp
from jax import lax
from jax.experimental import pallas as pl
from jax.experimental.pallas import tpu as pltpu
from jax.sharding import PartitionSpec as P

RBLK = 16
STEPS = 8
AHEAD = 2
MESH = pl.DeviceIdType.MESH


def kernel(
    reps,
    tps,
    steps,
    tokens,
    weight,
    factors_in,
    factors_out,
    adapter,
    scale,
    out,
    tok,
    w,
    fin,
    fout,
    base,
    acc,
    up,
    down,
    done,
    ask,
    asked,
    low,
    lows,
    spread,
    load_sem,
    own_sem,
    out_sem,
    tok_send,
    tok_fwd,
    tok_recv,
    a_send,
    a_recv,
    b_send,
    b_recv,
    c_send,
    c_recv,
    up_send,
    up_recv,
    down_send,
    down_recv,
):
    r = lax.axis_index("rep")
    t = lax.axis_index("tp")
    rows = tokens.shape[0]
    q = rows // steps
    width = weight.shape[1]
    tile = min(width, 512)
    in_share, out_share = fin.shape[0], fout.shape[0]
    rank = fin.shape[2]
    f32, bf16 = jnp.float32, jnp.bfloat16
    sibling = r + 1 - 2 * (r % 2)
    peers = [(r + 2 * j) % reps for j in range(1, reps // 2)]

    def remote(src, dst, send, recv, **where):
        return pltpu.make_async_remote_copy(
            src_ref=src, dst_ref=dst, send_sem=send, recv_sem=recv, device_id=where, device_id_type=MESH
        )

    loads = [
        pltpu.make_async_copy(src, dst, load_sem.at[i])
        for i, (src, dst) in enumerate(((factors_in, fin), (weight, w), (factors_out, fout)))
    ]
    for copy in loads:
        copy.start()

    def own(s):
        return pltpu.make_async_copy(tokens.at[pl.ds(s * q, q)], tok.at[s, r], own_sem.at[s])

    for s in range(steps):
        own(s).start()

    barrier = pltpu.get_barrier_semaphore()
    for j in range(1, reps):
        pl.semaphore_signal(barrier, inc=1, device_id={"rep": (r + j) % reps}, device_id_type=MESH)
    for j in range(1, tps):
        pl.semaphore_signal(barrier, inc=1, device_id={"tp": (t + j) % tps}, device_id_type=MESH)
    pl.semaphore_wait(barrier, reps + tps - 2)

    def token_copy(s, block, to, send, from_tokens):
        src = tokens.at[pl.ds(s * q, q)] if from_tokens else tok.at[s, block]
        return remote(src, tok.at[s, block], send, tok_recv.at[s, block], rep=to)

    def gather_start(s):
        for j, peer in enumerate(peers):
            token_copy(s, r, peer, tok_send.at[s, j], True).start()
        token_copy(s, r, sibling, tok_send.at[s, len(peers)], True).start()

    def gather_finish(s):
        own(s).wait()
        for j, peer in enumerate(peers):
            token_copy(s, peer, peer, tok_send.at[s, j], False).wait_recv()
            token_copy(s, peer, sibling, tok_fwd.at[s, j], False).start()
        token_copy(s, sibling, sibling, tok_send.at[s, len(peers)], False).wait_recv()
        for peer in peers:
            other = peer + 1 - 2 * (peer % 2)
            token_copy(s, other, sibling, tok_send.at[s, 0], False).wait_recv()

    def lowrank_ask(s):
        rowsall = tok[s].reshape(reps * q, tok.shape[3])
        chosen = jnp.zeros((reps * q, rank), f32)
        wanted = adapter[s].reshape(reps * q, rank) - r * in_share
        for n in range(in_share):
            product = jnp.dot(rowsall, fin[n], preferred_element_type=f32)
            chosen = jnp.where(wanted == n, product, chosen)
        ask[s] = chosen.astype(bf16).reshape(reps, q, rank)
        for j in range(1, reps):
            a_copy(s, (r + j) % reps, r, j).start()

    def a_copy(s, to, slot, j):
        return remote(ask.at[s, to], asked.at[s, slot], a_send.at[s, j], a_recv.at[s, slot], rep=to)

    def lowrank_sum(s):
        total = ask[s, r].astype(f32)
        for j in range(1, reps):
            peer = (r + j) % reps
            a_copy(s, peer, peer, j).wait_recv()
            total += asked[s, peer].astype(f32)
        lows[s, t] = total.astype(bf16)
        for j in range(1, tps):
            b_copy(s, (t + j) % tps, t, j).start()

    def b_copy(s, to, slot, j):
        return remote(lows.at[s, slot], lows.at[s, slot], b_send.at[s, j], b_recv.at[s, slot], tp=to)

    def lowrank_scale(s):
        for j in range(1, tps):
            peer = (t + j) % tps
            b_copy(s, peer, peer, j).wait_recv()
        total = lows[s, 0].astype(f32)
        for k in range(1, tps):
            total += lows[s, k].astype(f32)
        low[s, r] = (total * scale[s, r]).astype(bf16)
        for j in range(1, reps):
            c_copy(s, (r + j) % reps, r, j).start()

    def c_copy(s, to, slot, j):
        return remote(low.at[s, slot], low.at[s, slot], c_send.at[s, j], c_recv.at[s, slot], rep=to)

    def lowrank_wait(s):
        for j in range(1, reps):
            peer = (r + j) % reps
            c_copy(s, peer, peer, j).wait_recv()

    def project(s):
        @pl.loop(0, width // tile)
        def _(i):
            columns = pl.ds(pl.multiple_of(i * tile, tile), tile)
            base[:, columns] = jnp.dot(
                tok[s].reshape(reps * q, tok.shape[3]), w[:, columns], preferred_element_type=f32
            )

    def adapt(s):
        mine = adapter[s].reshape(reps * q, rank) - t * out_share
        value = low[s].reshape(reps * q, rank)
        for n in range(out_share):
            spread[:, n * rank : (n + 1) * rank] = jnp.where(
                mine == n, value.astype(f32), 0.0
            ).astype(bf16)

        @pl.loop(0, width // tile)
        def _(i):
            columns = pl.ds(pl.multiple_of(i * tile, tile), tile)
            block = fout[:, :, columns].reshape(out_share * rank, tile)
            delta = jnp.dot(spread[...], block, preferred_element_type=f32)
            acc[s, :, :, columns] = (base[:, columns] + delta).astype(bf16).reshape(tps, q, tile)

    def up_copy(s, src, b, to):
        return remote(src.at[s, b], up.at[s, b], up_send.at[s, b], up_recv.at[s, b], tp=to)

    def down_copy(s, src, b, to):
        return remote(src.at[s, b], down.at[s, b], down_send.at[s, b], down_recv.at[s, b], tp=to)

    above = jnp.minimum(t + 1, tps - 1)
    below = jnp.maximum(t - 1, 0)

    def ends_send(s, first, end):
        @pl.when(t == 0)
        def _():
            for k in range(first, end):
                up_copy(s, acc, tps - 1 - k, 1).start()

        @pl.when(t == tps - 1)
        def _():
            for k in range(first, end):
                down_copy(s, acc, k, tps - 2).start()

    def write(s):
        return pltpu.make_async_copy(done.at[s], out.at[pl.ds(pl.multiple_of(s * q, q), q)], out_sem.at[s])

    far = jnp.maximum(t, tps - 1 - t)

    def pass_on(slot):
        s_up, s_down, s_end = slot - t, slot - (tps - 1 - t), slot - far
        ups = (t > 0) & (s_up >= 0) & (s_up < steps)
        downs = (t < tps - 1) & (s_down >= 0) & (s_down < steps)

        @pl.loop(0, tps)
        def _(j):
            b = tps - 1 - j

            @pl.when(ups & (b > t))
            def _():
                up_copy(s_up, up, b, below).wait_recv()
                up[s_up, b] = (up[s_up, b].astype(f32) + acc[s_up, b].astype(f32)).astype(bf16)
                up_copy(s_up, up, b, above).start()

            @pl.when(downs & (j < t))
            def _():
                down_copy(s_down, down, j, above).wait_recv()
                down[s_down, j] = (
                    down[s_down, j].astype(f32) + acc[s_down, j].astype(f32)
                ).astype(bf16)
                down_copy(s_down, down, j, below).start()

        ended = (s_end >= 0) & (s_end < steps)

        @pl.when(ended & (t == 0))
        def _():
            down_copy(s_end, down, 0, 1).wait_recv()
            done[s_end] = (acc[s_end, 0].astype(f32) + down[s_end, 0].astype(f32)).astype(bf16)

        @pl.when(ended & (t == tps - 1))
        def _():
            up_copy(s_end, up, tps - 1, tps - 2).wait_recv()
            done[s_end] = (
                acc[s_end, tps - 1].astype(f32) + up[s_end, tps - 1].astype(f32)
            ).astype(bf16)

        @pl.when(ended & (t > 0) & (t < tps - 1))
        def _():
            up_copy(s_end, up, t, t - 1).wait_recv()
            down_copy(s_end, down, t, t + 1).wait_recv()
            done[s_end] = (
                acc[s_end, t].astype(f32) + up[s_end, t].astype(f32) + down[s_end, t].astype(f32)
            ).astype(bf16)

        @pl.when(ended)
        def _():
            write(s_end).start()

    def rows_in(s):
        if s < steps:
            gather_finish(s)
            if s + AHEAD < steps:
                gather_start(s + AHEAD)
            lowrank_ask(s)

    for s in range(min(AHEAD, steps)):
        gather_start(s)
    loads[0].wait()
    rows_in(0)
    rows_in(1)
    lowrank_sum(0)
    rows_in(2)
    lowrank_scale(0)
    if steps > 1:
        lowrank_sum(1)
    loads[1].wait()
    project(0)
    loads[2].wait()
    for s in range(steps):
        lowrank_wait(s)
        adapt(s)
        ends_send(s, 0, 1)
        if s + 2 < steps:
            lowrank_sum(s + 2)
        ends_send(s, 1, tps - 1)
        if s + 1 < steps:
            lowrank_scale(s + 1)
        rows_in(s + 3)
        if s + 1 < steps:
            project(s + 1)
        if s > 0:
            pass_on(s)

    @pl.loop(steps, steps + tps - 1)
    def _(slot):
        pass_on(slot)

    for s in range(steps):
        for j, peer in enumerate(peers):
            token_copy(s, r, peer, tok_send.at[s, j], True).wait_send()
            token_copy(s, peer, sibling, tok_fwd.at[s, j], False).wait_send()
        token_copy(s, r, sibling, tok_send.at[s, len(peers)], True).wait_send()
        for j in range(1, reps):
            a_copy(s, (r + j) % reps, r, j).wait_send()
            c_copy(s, (r + j) % reps, r, j).wait_send()
        for j in range(1, tps):
            b_copy(s, (t + j) % tps, t, j).wait_send()
        for b in range(tps):

            @pl.when(b > t)
            def _():
                up_copy(s, up, b, t + 1).wait_send()

            @pl.when(b < t)
            def _():
                down_copy(s, down, b, t - 1).wait_send()

        write(s).wait()


def body(reps, tps, tokens, weight, token_adapter_index, block_count, factors_in, factors_out):
    rows, depth = tokens.shape
    width = weight.shape[1]
    in_share, _, rank = factors_in.shape
    out_share = factors_out.shape[0]
    steps = STEPS
    q = rows // steps
    table = token_adapter_index[:, None] == jnp.arange(block_count.shape[0])[None, :]
    ranks = RBLK * jnp.sum(jnp.where(table, block_count[None, :], 0), axis=1)
    keep = jnp.arange(rank)[None, :] < ranks[:, None]
    scale = jnp.where(keep, (8.0 / jnp.sqrt(ranks.astype(jnp.float32)))[:, None], 0.0)
    adapter = jnp.broadcast_to(token_adapter_index[:, None], scale.shape)

    def by_step(x):
        return x.reshape(reps, steps, q, rank).transpose(1, 0, 2, 3)

    vmem = pl.BlockSpec(memory_space=pltpu.VMEM)
    hbm = pl.BlockSpec(memory_space=pl.ANY)
    f32, bf16 = jnp.float32, jnp.bfloat16
    dma = pltpu.SemaphoreType.DMA
    return pl.pallas_call(
        functools.partial(kernel, reps, tps, steps),
        out_shape=jax.ShapeDtypeStruct((rows, width), bf16),
        in_specs=[hbm, hbm, hbm, hbm, vmem, vmem],
        out_specs=hbm,
        scratch_shapes=[
            pltpu.VMEM((steps, reps, q, depth), bf16),
            pltpu.VMEM(weight.shape, bf16),
            pltpu.VMEM(factors_in.shape, bf16),
            pltpu.VMEM(factors_out.shape, bf16),
            pltpu.VMEM((reps * q, width), f32),
            pltpu.VMEM((steps, tps, q, width), bf16),
            pltpu.VMEM((steps, tps, q, width), bf16),
            pltpu.VMEM((steps, tps, q, width), bf16),
            pltpu.VMEM((steps, q, width), bf16),
            pltpu.VMEM((steps, reps, q, rank), bf16),
            pltpu.VMEM((steps, reps, q, rank), bf16),
            pltpu.VMEM((steps, reps, q, rank), bf16),
            pltpu.VMEM((steps, tps, q, rank), bf16),
            pltpu.VMEM((reps * q, out_share * rank), bf16),
            dma((3,)),
            dma((steps,)),
            dma((steps,)),
            dma((steps, reps)),
            dma((steps, reps)),
            dma((steps, reps)),
            dma((steps, reps)),
            dma((steps, reps)),
            dma((steps, tps)),
            dma((steps, tps)),
            dma((steps, reps)),
            dma((steps, reps)),
            dma((steps, tps)),
            dma((steps, tps)),
            dma((steps, tps)),
            dma((steps, tps)),
        ],
        compiler_params=pltpu.CompilerParams(
            collective_id=0, has_side_effects=True, vmem_limit_bytes=48 << 20
        ),
    )(tokens, weight, factors_in, factors_out, by_step(adapter), by_step(scale))


def solution(mesh):
    placed = (
        P(("parts", "rep"), "tp"),
        P("tp", "rep"),
        P("parts"),
        P(),
        P("rep", "tp", None),
        P("tp", None, "rep"),
    )
    return jax.shard_map(
        functools.partial(body, mesh.shape["rep"], mesh.shape["tp"]),
        mesh=mesh,
        in_specs=placed,
        out_specs=P(("parts", "tp"), "rep"),
        check_vma=False,
    )
```

```python
import functools

import jax
import jax.numpy as jnp
from jax import lax
from jax.experimental import pallas as pl
from jax.experimental.pallas import tpu as pltpu
from jax.sharding import PartitionSpec as P

RBLK = 16
STEPS = 8
AHEAD = 2
MESH = pl.DeviceIdType.MESH


def kernel(
    reps,
    tps,
    steps,
    tokens,
    weight,
    factors_in,
    factors_out,
    adapter,
    scale,
    out,
    tok,
    w,
    fin,
    fout,
    base,
    acc,
    up,
    down,
    done,
    ask,
    asked,
    low,
    lows,
    spread,
    load_sem,
    own_sem,
    out_sem,
    tok_send,
    tok_fwd,
    tok_recv,
    a_send,
    a_recv,
    b_send,
    b_recv,
    c_send,
    c_recv,
    up_send,
    up_recv,
    down_send,
    down_recv,
):
    r = lax.axis_index("rep")
    t = lax.axis_index("tp")
    rows = tokens.shape[0]
    q = rows // steps
    width = weight.shape[1]
    tile = min(width, 512)
    in_share, out_share = fin.shape[0], fout.shape[0]
    rank = fin.shape[2]
    f32, bf16 = jnp.float32, jnp.bfloat16
    sibling = r + 1 - 2 * (r % 2)
    peers = [(r + 2 * j) % reps for j in range(1, reps // 2)]

    def remote(src, dst, send, recv, **where):
        return pltpu.make_async_remote_copy(
            src_ref=src, dst_ref=dst, send_sem=send, recv_sem=recv, device_id=where, device_id_type=MESH
        )

    loads = [
        pltpu.make_async_copy(src, dst, load_sem.at[i])
        for i, (src, dst) in enumerate(((factors_in, fin), (weight, w), (factors_out, fout)))
    ]
    for copy in loads:
        copy.start()

    def own(s):
        return pltpu.make_async_copy(tokens.at[pl.ds(s * q, q)], tok.at[s, r], own_sem.at[s])

    for s in range(steps):
        own(s).start()

    barrier = pltpu.get_barrier_semaphore()
    for j in range(1, reps):
        pl.semaphore_signal(barrier, inc=1, device_id={"rep": (r + j) % reps}, device_id_type=MESH)
    for j in range(1, tps):
        pl.semaphore_signal(barrier, inc=1, device_id={"tp": (t + j) % tps}, device_id_type=MESH)
    pl.semaphore_wait(barrier, reps + tps - 2)

    def token_copy(s, block, to, send, from_tokens):
        src = tokens.at[pl.ds(s * q, q)] if from_tokens else tok.at[s, block]
        return remote(src, tok.at[s, block], send, tok_recv.at[s, block], rep=to)

    def gather_start(s):
        for j, peer in enumerate(peers):
            token_copy(s, r, peer, tok_send.at[s, j], True).start()
        token_copy(s, r, sibling, tok_send.at[s, len(peers)], True).start()

    def gather_finish(s):
        own(s).wait()
        for j, peer in enumerate(peers):
            token_copy(s, peer, peer, tok_send.at[s, j], False).wait_recv()
            token_copy(s, peer, sibling, tok_fwd.at[s, j], False).start()
        token_copy(s, sibling, sibling, tok_send.at[s, len(peers)], False).wait_recv()
        for peer in peers:
            other = peer + 1 - 2 * (peer % 2)
            token_copy(s, other, sibling, tok_send.at[s, 0], False).wait_recv()

    def lowrank_ask(s):
        rowsall = tok[s].reshape(reps * q, tok.shape[3])
        chosen = jnp.zeros((reps * q, rank), f32)
        wanted = adapter[s].reshape(reps * q, rank) - r * in_share
        for n in range(in_share):
            product = jnp.dot(rowsall, fin[n], preferred_element_type=f32)
            chosen = jnp.where(wanted == n, product, chosen)
        ask[s] = chosen.astype(bf16).reshape(reps, q, rank)
        for j in range(1, reps):
            a_copy(s, (r + j) % reps, r, j).start()

    def a_copy(s, to, slot, j):
        return remote(ask.at[s, to], asked.at[s, slot], a_send.at[s, j], a_recv.at[s, slot], rep=to)

    def lowrank_sum(s):
        total = ask[s, r].astype(f32)
        for j in range(1, reps):
            peer = (r + j) % reps
            a_copy(s, peer, peer, j).wait_recv()
            total += asked[s, peer].astype(f32)
        lows[s, t] = total.astype(bf16)
        for j in range(1, tps):
            b_copy(s, (t + j) % tps, t, j).start()

    def b_copy(s, to, slot, j):
        return remote(lows.at[s, slot], lows.at[s, slot], b_send.at[s, j], b_recv.at[s, slot], tp=to)

    def lowrank_scale(s):
        for j in range(1, tps):
            peer = (t + j) % tps
            b_copy(s, peer, peer, j).wait_recv()
        total = lows[s, 0].astype(f32)
        for k in range(1, tps):
            total += lows[s, k].astype(f32)
        low[s, r] = (total * scale[s, r]).astype(bf16)
        for j in range(1, reps):
            c_copy(s, (r + j) % reps, r, j).start()

    def c_copy(s, to, slot, j):
        return remote(low.at[s, slot], low.at[s, slot], c_send.at[s, j], c_recv.at[s, slot], rep=to)

    def lowrank_wait(s):
        for j in range(1, reps):
            peer = (r + j) % reps
            c_copy(s, peer, peer, j).wait_recv()

    def project(s):
        @pl.loop(0, width // tile)
        def _(i):
            columns = pl.ds(pl.multiple_of(i * tile, tile), tile)
            base[:, columns] = jnp.dot(
                tok[s].reshape(reps * q, tok.shape[3]), w[:, columns], preferred_element_type=f32
            )

    def adapt(s):
        mine = adapter[s].reshape(reps * q, rank) - t * out_share
        value = low[s].reshape(reps * q, rank)
        for n in range(out_share):
            spread[:, n * rank : (n + 1) * rank] = jnp.where(
                mine == n, value.astype(f32), 0.0
            ).astype(bf16)

        @pl.loop(0, width // tile)
        def _(i):
            columns = pl.ds(pl.multiple_of(i * tile, tile), tile)
            block = fout[:, :, columns].reshape(out_share * rank, tile)
            delta = jnp.dot(spread[...], block, preferred_element_type=f32)
            acc[s, :, :, columns] = (base[:, columns] + delta).astype(bf16).reshape(tps, q, tile)

    def up_copy(s, src, b, to):
        return remote(src.at[s, b], up.at[s, b], up_send.at[s, b], up_recv.at[s, b], tp=to)

    def down_copy(s, src, b, to):
        return remote(src.at[s, b], down.at[s, b], down_send.at[s, b], down_recv.at[s, b], tp=to)

    above = jnp.minimum(t + 1, tps - 1)
    below = jnp.maximum(t - 1, 0)

    def ends_send(s, first, end):
        @pl.when(t == 0)
        def _():
            for k in range(first, end):
                up_copy(s, acc, tps - 1 - k, 1).start()

        @pl.when(t == tps - 1)
        def _():
            for k in range(first, end):
                down_copy(s, acc, k, tps - 2).start()

    def write(s):
        return pltpu.make_async_copy(done.at[s], out.at[pl.ds(pl.multiple_of(s * q, q), q)], out_sem.at[s])

    far = jnp.maximum(t, tps - 1 - t)

    def pass_on(slot):
        s_up, s_down, s_end = slot - t, slot - (tps - 1 - t), slot - far
        ups = (t > 0) & (s_up >= 0) & (s_up < steps)
        downs = (t < tps - 1) & (s_down >= 0) & (s_down < steps)

        @pl.loop(0, tps)
        def _(j):
            b = tps - 1 - j

            @pl.when(ups & (b > t))
            def _():
                up_copy(s_up, up, b, below).wait_recv()
                up[s_up, b] = (up[s_up, b].astype(f32) + acc[s_up, b].astype(f32)).astype(bf16)
                up_copy(s_up, up, b, above).start()

            @pl.when(downs & (j < t))
            def _():
                down_copy(s_down, down, j, above).wait_recv()
                down[s_down, j] = (
                    down[s_down, j].astype(f32) + acc[s_down, j].astype(f32)
                ).astype(bf16)
                down_copy(s_down, down, j, below).start()

        ended = (s_end >= 0) & (s_end < steps)

        @pl.when(ended & (t == 0))
        def _():
            down_copy(s_end, down, 0, 1).wait_recv()
            done[s_end] = (acc[s_end, 0].astype(f32) + down[s_end, 0].astype(f32)).astype(bf16)

        @pl.when(ended & (t == tps - 1))
        def _():
            up_copy(s_end, up, tps - 1, tps - 2).wait_recv()
            done[s_end] = (
                acc[s_end, tps - 1].astype(f32) + up[s_end, tps - 1].astype(f32)
            ).astype(bf16)

        @pl.when(ended & (t > 0) & (t < tps - 1))
        def _():
            up_copy(s_end, up, t, t - 1).wait_recv()
            down_copy(s_end, down, t, t + 1).wait_recv()
            done[s_end] = (
                acc[s_end, t].astype(f32) + up[s_end, t].astype(f32) + down[s_end, t].astype(f32)
            ).astype(bf16)

        @pl.when(ended)
        def _():
            write(s_end).start()

    def rows_in(s):
        if s < steps:
            gather_finish(s)
            if s + AHEAD < steps:
                gather_start(s + AHEAD)
            lowrank_ask(s)

    for s in range(min(AHEAD, steps)):
        gather_start(s)
    loads[0].wait()
    rows_in(0)
    rows_in(1)
    lowrank_sum(0)
    loads[1].wait()
    project(0)
    lowrank_scale(0)
    if steps > 1:
        lowrank_sum(1)
    rows_in(2)
    loads[2].wait()
    for s in range(steps):
        lowrank_wait(s)
        adapt(s)
        ends_send(s, 0, 1)
        if s + 2 < steps:
            lowrank_sum(s + 2)
        ends_send(s, 1, tps - 1)
        if s + 1 < steps:
            lowrank_scale(s + 1)
        rows_in(s + 3)
        if s + 1 < steps:
            project(s + 1)
        if s > 0:
            pass_on(s)

    @pl.loop(steps, steps + tps - 1)
    def _(slot):
        pass_on(slot)

    for s in range(steps):
        for j, peer in enumerate(peers):
            token_copy(s, r, peer, tok_send.at[s, j], True).wait_send()
            token_copy(s, peer, sibling, tok_fwd.at[s, j], False).wait_send()
        token_copy(s, r, sibling, tok_send.at[s, len(peers)], True).wait_send()
        for j in range(1, reps):
            a_copy(s, (r + j) % reps, r, j).wait_send()
            c_copy(s, (r + j) % reps, r, j).wait_send()
        for j in range(1, tps):
            b_copy(s, (t + j) % tps, t, j).wait_send()
        for b in range(tps):

            @pl.when(b > t)
            def _():
                up_copy(s, up, b, t + 1).wait_send()

            @pl.when(b < t)
            def _():
                down_copy(s, down, b, t - 1).wait_send()

        write(s).wait()


def body(reps, tps, tokens, weight, token_adapter_index, block_count, factors_in, factors_out):
    rows, depth = tokens.shape
    width = weight.shape[1]
    in_share, _, rank = factors_in.shape
    out_share = factors_out.shape[0]
    steps = STEPS
    q = rows // steps
    table = token_adapter_index[:, None] == jnp.arange(block_count.shape[0])[None, :]
    ranks = RBLK * jnp.sum(jnp.where(table, block_count[None, :], 0), axis=1)
    keep = jnp.arange(rank)[None, :] < ranks[:, None]
    scale = jnp.where(keep, (8.0 / jnp.sqrt(ranks.astype(jnp.float32)))[:, None], 0.0)
    adapter = jnp.broadcast_to(token_adapter_index[:, None], scale.shape)

    def by_step(x):
        return x.reshape(reps, steps, q, rank).transpose(1, 0, 2, 3)

    vmem = pl.BlockSpec(memory_space=pltpu.VMEM)
    hbm = pl.BlockSpec(memory_space=pl.ANY)
    f32, bf16 = jnp.float32, jnp.bfloat16
    dma = pltpu.SemaphoreType.DMA
    return pl.pallas_call(
        functools.partial(kernel, reps, tps, steps),
        out_shape=jax.ShapeDtypeStruct((rows, width), bf16),
        in_specs=[hbm, hbm, hbm, hbm, vmem, vmem],
        out_specs=hbm,
        scratch_shapes=[
            pltpu.VMEM((steps, reps, q, depth), bf16),
            pltpu.VMEM(weight.shape, bf16),
            pltpu.VMEM(factors_in.shape, bf16),
            pltpu.VMEM(factors_out.shape, bf16),
            pltpu.VMEM((reps * q, width), f32),
            pltpu.VMEM((steps, tps, q, width), bf16),
            pltpu.VMEM((steps, tps, q, width), bf16),
            pltpu.VMEM((steps, tps, q, width), bf16),
            pltpu.VMEM((steps, q, width), bf16),
            pltpu.VMEM((steps, reps, q, rank), bf16),
            pltpu.VMEM((steps, reps, q, rank), bf16),
            pltpu.VMEM((steps, reps, q, rank), bf16),
            pltpu.VMEM((steps, tps, q, rank), bf16),
            pltpu.VMEM((reps * q, out_share * rank), bf16),
            dma((3,)),
            dma((steps,)),
            dma((steps,)),
            dma((steps, reps)),
            dma((steps, reps)),
            dma((steps, reps)),
            dma((steps, reps)),
            dma((steps, reps)),
            dma((steps, tps)),
            dma((steps, tps)),
            dma((steps, reps)),
            dma((steps, reps)),
            dma((steps, tps)),
            dma((steps, tps)),
            dma((steps, tps)),
            dma((steps, tps)),
        ],
        compiler_params=pltpu.CompilerParams(
            collective_id=0, has_side_effects=True, vmem_limit_bytes=63 << 20
        ),
    )(tokens, weight, factors_in, factors_out, by_step(adapter), by_step(scale))


def solution(mesh):
    placed = (
        P(("parts", "rep"), "tp"),
        P("tp", "rep"),
        P("parts"),
        P(),
        P("rep", "tp", None),
        P("tp", None, "rep"),
    )
    return jax.shard_map(
        functools.partial(body, mesh.shape["rep"], mesh.shape["tp"]),
        mesh=mesh,
        in_specs=placed,
        out_specs=P(("parts", "tp"), "rep"),
        check_vma=False,
    )
```
